32 devices in a mesh: member: 8 (over y, x, core), tile: 4 (over z).
Axes of the slice: x: 2, y: 2, z: 4, core: 2. Of those that a mesh axis runs over, the one named last changes fastest.
Arguments:
- state: float32 [8, 3, 4, 384, 512], P('member', None, None, 'tile'), may hold values from -6 to 6
- stiffness: float32 [4, 384, 512], P(None, 'tile'), may hold values from 0.1 to 0.45
- driver: float32 [16, 12, 512], P('tile', None, 'member'), may hold values from -6 to 6
- zone_rows: int32 [16], replicated, may hold values from 0 to 15, as said below
- zone_depth: int32 [8], P('member'), may hold values from 1 to 8, as said below
Outputs:
- advanced: float32 [8, 3, 4, 384, 512], P('member', None, None, 'tile')
The draws below stay inside these ranges and needn't reach their ends.
Inputs may be any that keep to these rules, and one draw needn't show every extreme that they name: `zone_rows`: the entries are a permutation of the zone rows; driver rows 0 to 7 carry the zone rows 8 to 15, the others the zone rows 0 to 7. `zone_depth`: some member has depth 8.
All inputs are finite; a program needn't handle non-finite values.
Results may differ from the reference program's by a relative error of at most 0.0003.
Values sent between devices are 32-bit elements; how exact they have to be, the bound alone decides.
A program may use at most 64 MiB of HBM per device.

```python
import math
import jax
import jax.numpy as jnp
from jax import lax

LEV = 4
NY = 512
ZONE = 8
SUBSTEPS = 3
MEMBERS = 8
NX = 384
ZROWS = 16


def draw_zone_rows(key, part):
    key = jax.random.fold_in(key, 11)
    first_key, second_key = jax.random.split(key)
    bottom_part = jax.random.permutation(first_key, ZONE) + ZONE
    top_part = jax.random.permutation(second_key, ZONE)
    return jnp.concatenate([bottom_part, top_part]).astype(jnp.int32)


def draw_zone_depth(key, part):
    key = jax.random.fold_in(key, 7)
    first_key, second_key = jax.random.split(key)
    depths = jax.random.randint(first_key, (MEMBERS,), 1, ZONE + 1)
    position = jax.random.randint(second_key, (), 0, MEMBERS)
    return depths.at[position].set(ZONE).astype(jnp.int32)


def level_of(stream_key, dims, cuts, least, largest):
    def one(dim, parts):
        draws = jax.random.uniform(jax.random.fold_in(jax.random.fold_in(stream_key, 6), dim), (parts,), jnp.float32, least / len(cuts), largest / len(cuts))
        return jnp.repeat(jnp.exp(draws), dims[dim] // parts).reshape((-1,) + (1,) * (len(dims) - dim - 1))

    gain = one(*cuts[0])
    for cut in cuts[1:]:
        gain = gain * one(*cut)
    return gain


def noise(rng, extent, width, bound, shards=(), kind=jnp.bfloat16):
    array = width * jax.random.normal(rng, extent, jnp.float32)
    if shards:
        array = array * level_of(rng, extent, shards, -0.22, 0.18)
    return jnp.clip(array, -bound, bound).astype(kind)


def setup_inputs(seed: int = 0) -> dict:
    keys = jax.random.split(jax.random.key(seed), 6)
    return {
        "state": noise(keys[0], (MEMBERS, 3, LEV, NX, NY), 1.0, 6.0, ((0, 8), (3, 4)), jnp.float32),
        "stiffness": jnp.clip(jnp.exp(math.log(0.45) - 1.50407736 * jax.random.uniform(keys[1], (LEV, NX, NY), jnp.float32) ** level_of(keys[1], (LEV, NX, NY), ((1, 4),), -0.2, 0.2)), 0.1, 0.45),
        "driver": noise(keys[2], (ZROWS, 3 * LEV, NY), 1.0, 6.0, ((0, 4), (2, 8)), jnp.float32),
        "zone_rows": draw_zone_rows(jax.random.fold_in(keys[5], 71), 0),
        "zone_depth": draw_zone_depth(jax.random.fold_in(keys[5], 71), 0),
    }


relax_peak = 0.9


def shift_down(field):
    return jnp.concatenate([jnp.zeros_like(field[..., :1, :]), field[..., :-1, :]], axis=-2)


def shift_up(field):
    return jnp.concatenate([field[..., 1:, :], jnp.zeros_like(field[..., :1, :])], axis=-2)


def reference(state, stiffness, driver, zone_rows, zone_depth):
    placed = jnp.zeros_like(driver).at[zone_rows].set(driver)
    zone_state = jnp.transpose(placed.reshape(ZROWS, 3, LEV, NY), (1, 2, 0, 3))
    top_target = zone_state[:, :, :ZONE]
    bottom_target = zone_state[:, :, ZONE:][:, :, ::-1]
    distance = jnp.arange(ZONE).astype(jnp.float32)

    def member(inputs):
        fields, depth = inputs
        depths = depth.astype(jnp.float32)
        ratio = (depths - distance) / depths
        top_weight = jnp.where(distance < depths, relax_peak * ratio * ratio, jnp.float32(0.0))
        bottom_weight = top_weight[::-1]
        pressure, along_x, along_y = fields[0], fields[1], fields[2]
        for substep in range(SUBSTEPS):
            pressure = pressure - stiffness * ((along_x - shift_down(along_x)) + (along_y - jnp.roll(along_y, 1, -1)))
            along_x = along_x - (shift_up(pressure) - pressure)
            along_y = along_y - (jnp.roll(pressure, -1, -1) - pressure)
            stacked = jnp.stack([pressure, along_x, along_y])
            top_part = stacked[:, :, :ZONE]
            top_part = top_part + top_weight[:, None] * (top_target - top_part)
            bottom_part = stacked[:, :, NX - ZONE:]
            bottom_part = bottom_part + bottom_weight[:, None] * (bottom_target - bottom_part)
            stacked = stacked.at[:, :, :ZONE].set(top_part)
            stacked = stacked.at[:, :, NX - ZONE:].set(bottom_part)
            pressure, along_x, along_y = stacked[0], stacked[1], stacked[2]
        return jnp.stack([pressure, along_x, along_y])

    return lax.map(member, (state, zone_depth))
```

```python
import functools

import jax
import jax.numpy as jnp
from jax import lax
from jax.experimental import pallas as pl
from jax.experimental.pallas import tpu as pltpu
from jax.sharding import PartitionSpec as P

ZONE = 8
SUBSTEPS = 3
HALO = 3
TILE = 8
LANES = 128

relax_peak = 0.9


def rotated(field, amount, axis):
    return pltpu.roll(field, amount % field.shape[axis], axis)


def sweep(load, emit, tiles, relax, keep):
    columns = None
    pending = [None] * SUBSTEPS

    def finish(stage, above):
        index, stiff, new_pressure, along_x, new_y = pending[stage]
        row = lax.broadcasted_iota(jnp.int32, new_pressure.shape, 0)
        turned = rotated(new_pressure, -1, 0)
        if above is not None:
            turned = jnp.where(row == TILE - 1, rotated(above, -1, 0), turned)
        new_x = along_x - (turned - new_pressure)
        fields = [new_pressure, new_x, new_y]
        if relax is not None and index == 1:
            weight, targets = relax
            fields = [f + weight * (b - f) for f, b in zip(fields, targets)]
        if keep is not None and index == 0:
            fields[1] = fields[1] * keep
        push(stage + 1, index, stiff, fields)

    def push(stage, index, stiff, fields):
        if stage == SUBSTEPS:
            emit(index, fields)
            return
        pressure, along_x, along_y = fields
        row = lax.broadcasted_iota(jnp.int32, pressure.shape, 0)
        turned = rotated(along_x, 1, 0)
        before = pending[stage]
        if before is not None:
            turned = jnp.where(row == 0, rotated(before[3], 1, 0), turned)
        flow = (along_x - turned) + (along_y - rotated(along_y, 1, 1))
        new_pressure = pressure - stiff * flow
        new_y = along_y - (rotated(new_pressure, -1, 1) - new_pressure)
        if before is not None:
            finish(stage, new_pressure)
        pending[stage] = (index, stiff, new_pressure, along_x, new_y)

    for index in range(tiles):
        stiff, fields = load(index)
        push(0, index, stiff, fields)
    for stage in range(SUBSTEPS):
        finish(stage, None)


def kernel(members, tiles, zone_rows, zone_depth, state, stiffness, driver, out,
           fields, stiff, pieces, zone, load_sem, stiff_sem,
           up_send, up_recv, down_send, down_recv, piece_send, piece_recv, zone_send, zone_recv):
    levels, rows, columns = stiffness.shape
    _, parts, width = driver.shape
    per_group = LANES // width
    groups = members // per_group
    sources = tiles // 2
    per_source = driver.shape[0]
    member = lax.axis_index("member")
    tile = lax.axis_index("tile")
    bottom = tile == 0
    top = tile == tiles - 1
    edge = jnp.logical_or(bottom, top)
    group = member // per_group
    lane = member % per_group

    def at(member_to, tile_to):
        return {"member": member_to, "tile": tile_to}

    def loads(level):
        return pltpu.make_async_copy(
            state.at[0, :, level], fields.at[:, level, pl.ds(TILE, rows)], load_sem.at[level])

    stiff_load = pltpu.make_async_copy(stiffness, stiff.at[:, pl.ds(TILE, rows)], stiff_sem)

    barrier = pltpu.get_barrier_semaphore()

    def greet(device):
        pl.semaphore_signal(barrier, inc=1, device_id=device, device_id_type=pl.DeviceIdType.MESH)

    @pl.when(tile > 0)
    def _():
        greet(at(member, tile - 1))

    @pl.when(tile < tiles - 1)
    def _():
        greet(at(member, tile + 1))

    @pl.when(edge)
    def _():
        first = jnp.where(bottom, sources, 0)
        for s in range(sources):
            for g in range(per_group):
                greet(at(group * per_group + g, first + s))
        for j in range(1, groups):
            greet(at(lax.rem(group + j, groups) * per_group + lane, tile))

    stiff_load.start()
    for level in range(levels):
        loads(level).start()

    @pl.when(bottom)
    def _():
        fields[:, :, :TILE, :] = jnp.zeros((3, levels, TILE, columns), jnp.float32)
        stiff[:, :TILE, :] = jnp.zeros((levels, TILE, columns), jnp.float32)

    @pl.when(top)
    def _():
        fields[:, :, TILE + rows:, :] = jnp.zeros((3, levels, TILE, columns), jnp.float32)
        stiff[:, TILE + rows:, :] = jnp.zeros((levels, TILE, columns), jnp.float32)

    @pl.when(jnp.logical_not(edge))
    def _():
        zone[...] = jnp.zeros(zone.shape, jnp.float32)

    expected = per_group + jnp.where(bottom, 0, 1) + jnp.where(top, 0, 1)
    expected = expected + jnp.where(edge, groups - 1, 0)
    pl.semaphore_wait(barrier, expected)

    def remote(source, target, send, recv, device):
        return pltpu.make_async_remote_copy(
            src_ref=source, dst_ref=target, send_sem=send, recv_sem=recv,
            device_id=device, device_id_type=pl.DeviceIdType.MESH)

    def ups():
        device = at(member, tile + 1)
        copies = []
        for field, count in ((0, HALO - 1), (1, HALO), (2, HALO - 1)):
            copies.append(remote(
                state.at[0, field, :, pl.ds(rows - count, count)],
                fields.at[field, :, pl.ds(TILE - count, count)],
                up_send.at[field], up_recv.at[field], device))
        count = HALO - 1
        copies.append(remote(
            stiffness.at[:, pl.ds(rows - count, count)], stiff.at[:, pl.ds(TILE - count, count)],
            up_send.at[3], up_recv.at[3], device))
        return copies

    def downs():
        device = at(member, tile - 1)
        return [
            remote(state.at[0, :, :, pl.ds(0, HALO)], fields.at[:, :, pl.ds(TILE + rows, HALO)],
                   down_send.at[0], down_recv.at[0], device),
            remote(stiffness.at[:, pl.ds(0, HALO)], stiff.at[:, pl.ds(TILE + rows, HALO)],
                   down_send.at[1], down_recv.at[1], device),
        ]

    def piece(g, source_slot, lane_slot):
        target = jnp.where(tile < sources, tiles - 1, 0)
        return remote(driver, pieces.at[source_slot, lane_slot], piece_send.at[g],
                      piece_recv.at[source_slot, lane_slot], at(group * per_group + g, target))

    def zone_copy(j, slot):
        device = at(lax.rem(group + j, groups) * per_group + lane, tile)
        return remote(zone.at[slot], zone.at[slot], zone_send.at[j - 1], zone_recv.at[slot], device)

    my_slot = lax.rem(tile, sources)
    for g in range(per_group):
        piece(g, my_slot, lane).start()

    @pl.when(tile < tiles - 1)
    def _():
        for copy in ups():
            copy.start()

    @pl.when(tile > 0)
    def _():
        for copy in downs():
            copy.start()

    stiff_load.wait()

    def interior(level, carry):
        loads(level).wait()

        def load(index):
            at_rows = pl.ds(2 * TILE + TILE * index, TILE)
            return stiff[level, at_rows, :], [fields[f, level, at_rows, :] for f in range(3)]

        def emit(index, values):
            for f in range(3):
                out[0, f, level, pl.ds(TILE + TILE * index, TILE), :] = values[f]

        sweep(load, emit, rows // TILE - 2, None, None)
        return carry

    split = levels // 2
    lax.fori_loop(0, split, interior, 0)

    @pl.when(edge)
    def _():
        first = jnp.where(bottom, ZONE, 0)
        row = lax.broadcasted_iota(jnp.int32, (TILE, LANES), 0)
        wanted = jnp.where(bottom, row, 2 * ZONE - 1 - row)
        for s in range(sources):
            for g in range(per_group):
                piece(0, s, g).wait_recv()
        held = [jnp.zeros((TILE, LANES), jnp.float32) for _ in range(parts)]
        for s in range(sources):
            for r in range(per_source):
                chosen = wanted == zone_rows[first + s * per_source + r]
                block = jnp.concatenate([pieces[s, g, r] for g in range(per_group)], axis=-1)
                for part in range(parts):
                    held[part] = jnp.where(chosen, block[part:part + 1, :], held[part])
        for part in range(parts):
            zone[group, part] = held[part]
        for j in range(1, groups):
            zone_copy(j, group).start()

    lax.fori_loop(split, levels, interior, 0)

    row = lax.broadcasted_iota(jnp.int32, (TILE, columns), 0)
    depth = zone_depth[0].astype(jnp.float32)

    def weights(distance, here):
        distance = distance.astype(jnp.float32)
        ratio = (depth - distance) / depth
        return jnp.where(jnp.logical_and(here, distance < depth), relax_peak * ratio * ratio, 0.0)

    low_weight = weights(row, bottom)
    high_weight = weights(ZONE - 1 - row, top)
    keep = jnp.where(bottom, 0.0, 1.0).astype(jnp.float32)

    @pl.when(tile > 0)
    def _():
        for copy in ups():
            copy.wait_recv()

    @pl.when(tile < tiles - 1)
    def _():
        for copy in downs():
            copy.wait_recv()

    @pl.when(edge)
    def _():
        for j in range(1, groups):
            zone_copy(j, lax.rem(group + groups - j, groups)).wait_recv()

    def strips(level, carry):
        def targets():
            return [jnp.concatenate([zone[g, f * levels + level] for g in range(groups)], axis=-1)
                    for f in range(3)]

        def strip(base, weight, keep, emit):
            def load(index):
                at_rows = pl.ds(base + TILE * index, TILE)
                return stiff[level, at_rows, :], [fields[f, level, at_rows, :] for f in range(3)]

            sweep(load, emit, 3, (weight, targets()), keep)

        def emit_low(index, values):
            for f in range(3):
                if index == 1:
                    out[0, f, level, pl.ds(0, TILE), :] = values[f]
                if index == 2:
                    out[0, f, level, pl.ds(TILE, HALO), :] = values[f][:HALO]

        def emit_high(index, values):
            for f in range(3):
                if index == 0:
                    out[0, f, level, pl.ds(rows - TILE - HALO, HALO), :] = values[f][TILE - HALO:]
                if index == 1:
                    out[0, f, level, pl.ds(rows - TILE, TILE), :] = values[f]

        strip(0, low_weight, keep, emit_low)
        strip(rows - TILE, high_weight, None, emit_high)
        return carry

    lax.fori_loop(0, levels, strips, 0)

    @pl.when(tile < tiles - 1)
    def _():
        for copy in ups():
            copy.wait_send()

    @pl.when(tile > 0)
    def _():
        for copy in downs():
            copy.wait_send()

    for g in range(per_group):
        piece(g, my_slot, lane).wait_send()

    @pl.when(edge)
    def _():
        for j in range(1, groups):
            zone_copy(j, group).wait_send()


def body(state, stiffness, driver, zone_rows, zone_depth):
    members = lax.axis_size("member")
    tiles = lax.axis_size("tile")
    levels, rows, columns = stiffness.shape
    parts, width = driver.shape[1:]
    per_group = LANES // width
    groups = members // per_group
    dma = pltpu.SemaphoreType.DMA
    padded = rows + 2 * TILE
    return pl.pallas_call(
        functools.partial(kernel, members, tiles),
        out_shape=jax.ShapeDtypeStruct(state.shape, jnp.float32),
        in_specs=[pl.BlockSpec(memory_space=pltpu.SMEM)] * 2
        + [pl.BlockSpec(memory_space=pl.ANY)] * 3,
        out_specs=pl.BlockSpec(memory_space=pltpu.VMEM),
        scratch_shapes=[
            pltpu.VMEM((3, levels, padded, columns), jnp.float32),
            pltpu.VMEM((levels, padded, columns), jnp.float32),
            pltpu.VMEM((tiles // 2, per_group) + driver.shape, jnp.float32),
            pltpu.VMEM((groups, parts, TILE, LANES), jnp.float32),
            dma((levels,)),
            dma,
            dma((4,)),
            dma((4,)),
            dma((2,)),
            dma((2,)),
            dma((per_group,)),
            dma((tiles // 2, per_group)),
            dma((groups,)),
            dma((groups,)),
        ],
        compiler_params=pltpu.CompilerParams(
            collective_id=0, has_side_effects=True, vmem_limit_bytes=40 * 2**20),
        name="substeps",
    )(zone_rows, zone_depth, state, stiffness, driver)


def solution(mesh):
    in_specs = (
        P("member", None, None, "tile", None),
        P(None, "tile", None),
        P("tile", None, "member"),
        P(),
        P("member"),
    )
    out_specs = P("member", None, None, "tile", None)
    return jax.shard_map(body, mesh=mesh, in_specs=in_specs, out_specs=out_specs, check_vma=False)
```

```python
import functools

import jax
import jax.numpy as jnp
from jax import lax
from jax.experimental import pallas as pl
from jax.experimental.pallas import tpu as pltpu
from jax.sharding import PartitionSpec as P

ZONE = 8
SUBSTEPS = 3
HALO = 3
TILE = 8
LANES = 128

relax_peak = 0.9


def rotated(field, amount, axis):
    return pltpu.roll(field, amount % field.shape[axis], axis)


def sweep(load, emit, tiles, relax, keep):
    columns = None
    pending = [None] * SUBSTEPS

    def finish(stage, above):
        index, stiff, new_pressure, along_x, new_y = pending[stage]
        row = lax.broadcasted_iota(jnp.int32, new_pressure.shape, 0)
        turned = rotated(new_pressure, -1, 0)
        if above is not None:
            turned = jnp.where(row == TILE - 1, rotated(above, -1, 0), turned)
        new_x = along_x - (turned - new_pressure)
        fields = [new_pressure, new_x, new_y]
        if relax is not None and index == 1:
            weight, targets = relax
            fields = [f + weight * (b - f) for f, b in zip(fields, targets)]
        if keep is not None and index == 0:
            fields[1] = fields[1] * keep
        push(stage + 1, index, stiff, fields)

    def push(stage, index, stiff, fields):
        if stage == SUBSTEPS:
            emit(index, fields)
            return
        pressure, along_x, along_y = fields
        row = lax.broadcasted_iota(jnp.int32, pressure.shape, 0)
        turned = rotated(along_x, 1, 0)
        before = pending[stage]
        if before is not None:
            turned = jnp.where(row == 0, rotated(before[3], 1, 0), turned)
        flow = (along_x - turned) + (along_y - rotated(along_y, 1, 1))
        new_pressure = pressure - stiff * flow
        new_y = along_y - (rotated(new_pressure, -1, 1) - new_pressure)
        if before is not None:
            finish(stage, new_pressure)
        pending[stage] = (index, stiff, new_pressure, along_x, new_y)

    for index in range(tiles):
        stiff, fields = load(index)
        push(0, index, stiff, fields)
    for stage in range(SUBSTEPS):
        finish(stage, None)


def kernel(members, tiles, zone_depth, zone_rows_hbm, state, stiffness, driver, out,
           zone_rows, rows_sem, fields, stiff, pieces, zone, load_sem, stiff_sem,
           up_send, up_recv, down_send, down_recv, piece_send, piece_recv, zone_send, zone_recv):
    levels, rows, columns = stiffness.shape
    parts, per_source, width = driver.shape
    per_group = LANES // width
    groups = members // per_group
    sources = tiles // 2
    member = lax.axis_index("member")
    tile = lax.axis_index("tile")
    bottom = tile == 0
    top = tile == tiles - 1
    edge = jnp.logical_or(bottom, top)
    group = member // per_group
    lane = member % per_group

    def at(member_to, tile_to):
        return {"member": member_to, "tile": tile_to}

    def loads(level):
        return pltpu.make_async_copy(
            state.at[0, :, level], fields.at[:, level, pl.ds(TILE, rows)], load_sem.at[level])

    stiff_load = pltpu.make_async_copy(stiffness, stiff.at[:, pl.ds(TILE, rows)], stiff_sem)

    barrier = pltpu.get_barrier_semaphore()

    def greet(device):
        pl.semaphore_signal(barrier, inc=1, device_id=device, device_id_type=pl.DeviceIdType.MESH)

    @pl.when(tile > 0)
    def _():
        greet(at(member, tile - 1))

    @pl.when(tile < tiles - 1)
    def _():
        greet(at(member, tile + 1))

    @pl.when(edge)
    def _():
        first = jnp.where(bottom, sources, 0)
        for s in range(sources):
            for g in range(per_group):
                greet(at(group * per_group + g, first + s))
        for j in range(1, groups):
            greet(at(lax.rem(group + j, groups) * per_group + lane, tile))

    rows_load = pltpu.make_async_copy(zone_rows_hbm, zone_rows, rows_sem)
    stiff_load.start()
    for level in range(levels):
        loads(level).start()
    rows_load.start()

    @pl.when(bottom)
    def _():
        fields[:, :, :TILE, :] = jnp.zeros((3, levels, TILE, columns), jnp.float32)
        stiff[:, :TILE, :] = jnp.zeros((levels, TILE, columns), jnp.float32)

    @pl.when(top)
    def _():
        fields[:, :, TILE + rows:, :] = jnp.zeros((3, levels, TILE, columns), jnp.float32)
        stiff[:, TILE + rows:, :] = jnp.zeros((levels, TILE, columns), jnp.float32)

    @pl.when(jnp.logical_not(edge))
    def _():
        zone[...] = jnp.zeros(zone.shape, jnp.float32)

    expected = per_group + jnp.where(bottom, 0, 1) + jnp.where(top, 0, 1)
    expected = expected + jnp.where(edge, groups - 1, 0)
    pl.semaphore_wait(barrier, expected)

    def remote(source, target, send, recv, device):
        return pltpu.make_async_remote_copy(
            src_ref=source, dst_ref=target, send_sem=send, recv_sem=recv,
            device_id=device, device_id_type=pl.DeviceIdType.MESH)

    def ups():
        device = at(member, tile + 1)
        copies = []
        for field, count in ((0, HALO - 1), (1, HALO), (2, HALO - 1)):
            copies.append(remote(
                state.at[0, field, :, pl.ds(rows - count, count)],
                fields.at[field, :, pl.ds(TILE - count, count)],
                up_send.at[field], up_recv.at[field], device))
        count = HALO - 1
        copies.append(remote(
            stiffness.at[:, pl.ds(rows - count, count)], stiff.at[:, pl.ds(TILE - count, count)],
            up_send.at[3], up_recv.at[3], device))
        return copies

    def downs():
        device = at(member, tile - 1)
        return [
            remote(state.at[0, :, :, pl.ds(0, HALO)], fields.at[:, :, pl.ds(TILE + rows, HALO)],
                   down_send.at[0], down_recv.at[0], device),
            remote(stiffness.at[:, pl.ds(0, HALO)], stiff.at[:, pl.ds(TILE + rows, HALO)],
                   down_send.at[1], down_recv.at[1], device),
        ]

    def piece(g, source_slot, lane_slot):
        target = jnp.where(tile < sources, tiles - 1, 0)
        return remote(driver, pieces.at[source_slot, lane_slot], piece_send.at[g],
                      piece_recv.at[source_slot, lane_slot], at(group * per_group + g, target))

    def zone_copy(j, slot):
        device = at(lax.rem(group + j, groups) * per_group + lane, tile)
        return remote(zone.at[slot], zone.at[slot], zone_send.at[j - 1], zone_recv.at[slot], device)

    my_slot = lax.rem(tile, sources)
    for g in range(per_group):
        piece(g, my_slot, lane).start()

    @pl.when(tile < tiles - 1)
    def _():
        for copy in ups():
            copy.start()

    @pl.when(tile > 0)
    def _():
        for copy in downs():
            copy.start()

    stiff_load.wait()
    rows_load.wait()

    def interior(level, carry):
        loads(level).wait()

        def load(index):
            at_rows = pl.ds(2 * TILE + TILE * index, TILE)
            return stiff[level, at_rows, :], [fields[f, level, at_rows, :] for f in range(3)]

        def emit(index, values):
            for f in range(3):
                out[0, f, level, pl.ds(TILE + TILE * index, TILE), :] = values[f]

        sweep(load, emit, rows // TILE - 2, None, None)
        return carry

    split = levels // 2
    lax.fori_loop(0, split, interior, 0)

    @pl.when(edge)
    def _():
        first = jnp.where(bottom, ZONE, 0)
        row = lax.broadcasted_iota(jnp.int32, (TILE, LANES), 0)
        wanted = jnp.where(bottom, row, 2 * ZONE - 1 - row)
        for s in range(sources):
            for g in range(per_group):
                piece(0, s, g).wait_recv()
        held = [jnp.zeros((TILE, LANES), jnp.float32) for _ in range(parts)]
        for s in range(sources):
            chosen = [wanted == zone_rows[first + s * per_source + r] for r in range(per_source)]
            for part in range(parts):
                block = jnp.concatenate([pieces[s, g, part] for g in range(per_group)], axis=-1)
                for r in range(per_source):
                    held[part] = jnp.where(chosen[r], block[r:r + 1, :], held[part])
        for part in range(parts):
            zone[group, part] = held[part]
        for j in range(1, groups):
            zone_copy(j, group).start()

    lax.fori_loop(split, levels, interior, 0)

    row = lax.broadcasted_iota(jnp.int32, (TILE, columns), 0)
    depth = zone_depth[0].astype(jnp.float32)

    def weights(distance, here):
        distance = distance.astype(jnp.float32)
        ratio = (depth - distance) / depth
        return jnp.where(jnp.logical_and(here, distance < depth), relax_peak * ratio * ratio, 0.0)

    low_weight = weights(row, bottom)
    high_weight = weights(ZONE - 1 - row, top)
    keep = jnp.where(bottom, 0.0, 1.0).astype(jnp.float32)

    @pl.when(tile > 0)
    def _():
        for copy in ups():
            copy.wait_recv()

    @pl.when(tile < tiles - 1)
    def _():
        for copy in downs():
            copy.wait_recv()

    @pl.when(edge)
    def _():
        for j in range(1, groups):
            zone_copy(j, lax.rem(group + groups - j, groups)).wait_recv()

    def strips(level, carry):
        def targets():
            return [jnp.concatenate([zone[g, f * levels + level] for g in range(groups)], axis=-1)
                    for f in range(3)]

        def strip(base, weight, keep, emit):
            def load(index):
                at_rows = pl.ds(base + TILE * index, TILE)
                return stiff[level, at_rows, :], [fields[f, level, at_rows, :] for f in range(3)]

            sweep(load, emit, 3, (weight, targets()), keep)

        def emit_low(index, values):
            for f in range(3):
                if index == 1:
                    out[0, f, level, pl.ds(0, TILE), :] = values[f]
                if index == 2:
                    out[0, f, level, pl.ds(TILE, HALO), :] = values[f][:HALO]

        def emit_high(index, values):
            for f in range(3):
                if index == 0:
                    out[0, f, level, pl.ds(rows - TILE - HALO, HALO), :] = values[f][TILE - HALO:]
                if index == 1:
                    out[0, f, level, pl.ds(rows - TILE, TILE), :] = values[f]

        strip(0, low_weight, keep, emit_low)
        strip(rows - TILE, high_weight, None, emit_high)
        return carry

    lax.fori_loop(0, levels, strips, 0)

    @pl.when(tile < tiles - 1)
    def _():
        for copy in ups():
            copy.wait_send()

    @pl.when(tile > 0)
    def _():
        for copy in downs():
            copy.wait_send()

    for g in range(per_group):
        piece(g, my_slot, lane).wait_send()

    @pl.when(edge)
    def _():
        for j in range(1, groups):
            zone_copy(j, group).wait_send()


def body(state, stiffness, driver, zone_rows, zone_depth):
    members = lax.axis_size("member")
    tiles = lax.axis_size("tile")
    levels, rows, columns = stiffness.shape
    driver = jnp.transpose(driver, (1, 0, 2))
    parts, _, width = driver.shape
    per_group = LANES // width
    groups = members // per_group
    dma = pltpu.SemaphoreType.DMA
    padded = rows + 2 * TILE
    operands = [pltpu.with_memory_space_constraint(operand, pltpu.HBM)
                for operand in (zone_rows, state, stiffness, driver)]
    return pl.pallas_call(
        functools.partial(kernel, members, tiles),
        out_shape=jax.ShapeDtypeStruct(state.shape, jnp.float32),
        in_specs=[pl.BlockSpec(memory_space=pltpu.SMEM)]
        + [pl.BlockSpec(memory_space=pltpu.HBM)] * 4,
        out_specs=pl.BlockSpec(memory_space=pltpu.VMEM),
        scratch_shapes=[
            pltpu.SMEM(zone_rows.shape, jnp.int32),
            dma,
            pltpu.VMEM((3, levels, padded, columns), jnp.float32),
            pltpu.VMEM((levels, padded, columns), jnp.float32),
            pltpu.VMEM((tiles // 2, per_group) + driver.shape, jnp.float32),
            pltpu.VMEM((groups, parts, TILE, LANES), jnp.float32),
            dma((levels,)),
            dma,
            dma((4,)),
            dma((4,)),
            dma((2,)),
            dma((2,)),
            dma((per_group,)),
            dma((tiles // 2, per_group)),
            dma((groups,)),
            dma((groups,)),
        ],
        compiler_params=pltpu.CompilerParams(
            collective_id=0, has_side_effects=True, vmem_limit_bytes=40 * 2**20),
        name="substeps",
    )(zone_depth, *operands)


def solution(mesh):
    in_specs = (
        P("member", None, None, "tile", None),
        P(None, "tile", None),
        P("tile", None, "member"),
        P(),
        P("member"),
    )
    out_specs = P("member", None, None, "tile", None)
    return jax.shard_map(body, mesh=mesh, in_specs=in_specs, out_specs=out_specs, check_vma=False)
```

```python
import functools

import jax
import jax.numpy as jnp
from jax import lax
from jax.experimental import pallas as pl
from jax.experimental.pallas import tpu as pltpu
from jax.sharding import PartitionSpec as P

ZONE = 8
SUBSTEPS = 3
HALO = 3
TILE = 8
LANES = 128

relax_peak = 0.9


def rotated(field, amount, axis):
    return pltpu.roll(field, amount % field.shape[axis], axis)


def sweep(load, emit, tiles, relax, keep):
    columns = None
    pending = [None] * SUBSTEPS

    def finish(stage, above):
        index, stiff, new_pressure, along_x, new_y = pending[stage]
        row = lax.broadcasted_iota(jnp.int32, new_pressure.shape, 0)
        turned = rotated(new_pressure, -1, 0)
        if above is not None:
            turned = jnp.where(row == TILE - 1, rotated(above, -1, 0), turned)
        new_x = along_x - (turned - new_pressure)
        fields = [new_pressure, new_x, new_y]
        if relax is not None and index == 1:
            weight, targets = relax
            fields = [f + weight * (b - f) for f, b in zip(fields, targets)]
        if keep is not None and index == 0:
            fields[1] = fields[1] * keep
        push(stage + 1, index, stiff, fields)

    def push(stage, index, stiff, fields):
        if stage == SUBSTEPS:
            emit(index, fields)
            return
        pressure, along_x, along_y = fields
        row = lax.broadcasted_iota(jnp.int32, pressure.shape, 0)
        turned = rotated(along_x, 1, 0)
        before = pending[stage]
        if before is not None:
            turned = jnp.where(row == 0, rotated(before[3], 1, 0), turned)
        flow = (along_x - turned) + (along_y - rotated(along_y, 1, 1))
        new_pressure = pressure - stiff * flow
        new_y = along_y - (rotated(new_pressure, -1, 1) - new_pressure)
        if before is not None:
            finish(stage, new_pressure)
        pending[stage] = (index, stiff, new_pressure, along_x, new_y)

    for index in range(tiles):
        stiff, fields = load(index)
        push(0, index, stiff, fields)
    for stage in range(SUBSTEPS):
        finish(stage, None)


def kernel(members, tiles, zone_depth, zone_rows_hbm, state, stiffness, driver, out,
           zone_rows, rows_sem, fields, stiff, own, packed, pieces, zone,
           load_sem, stiff_sem, own_sem,
           up_send, up_recv, down_send, down_recv, piece_send, piece_recv, zone_send, zone_recv):
    levels, rows, columns = stiffness.shape
    parts, per_source, width = driver.shape
    per_group = LANES // width
    groups = members // per_group
    sources = tiles // 2
    member = lax.axis_index("member")
    tile = lax.axis_index("tile")
    bottom = tile == 0
    top = tile == tiles - 1
    edge = jnp.logical_or(bottom, top)
    group = member // per_group
    lane = member % per_group

    def at(member_to, tile_to):
        return {"member": member_to, "tile": tile_to}

    def loads(level):
        return pltpu.make_async_copy(
            state.at[0, :, level], fields.at[:, level, pl.ds(TILE, rows)], load_sem.at[level])

    stiff_load = pltpu.make_async_copy(stiffness, stiff.at[:, pl.ds(TILE, rows)], stiff_sem)

    barrier = pltpu.get_barrier_semaphore()

    def greet(device):
        pl.semaphore_signal(barrier, inc=1, device_id=device, device_id_type=pl.DeviceIdType.MESH)

    @pl.when(tile > 0)
    def _():
        greet(at(member, tile - 1))

    @pl.when(tile < tiles - 1)
    def _():
        greet(at(member, tile + 1))

    @pl.when(edge)
    def _():
        first = jnp.where(bottom, sources, 0)
        for s in range(sources):
            for g in range(per_group):
                greet(at(group * per_group + g, first + s))
        for j in range(1, groups):
            greet(at(lax.rem(group + j, groups) * per_group + lane, tile))

    own_load = pltpu.make_async_copy(driver, own, own_sem)
    rows_load = pltpu.make_async_copy(zone_rows_hbm, zone_rows, rows_sem)
    own_load.start()
    stiff_load.start()
    for level in range(levels):
        loads(level).start()
    rows_load.start()

    @pl.when(bottom)
    def _():
        fields[:, :, :TILE, :] = jnp.zeros((3, levels, TILE, columns), jnp.float32)
        stiff[:, :TILE, :] = jnp.zeros((levels, TILE, columns), jnp.float32)

    @pl.when(top)
    def _():
        fields[:, :, TILE + rows:, :] = jnp.zeros((3, levels, TILE, columns), jnp.float32)
        stiff[:, TILE + rows:, :] = jnp.zeros((levels, TILE, columns), jnp.float32)

    @pl.when(jnp.logical_not(edge))
    def _():
        zone[...] = jnp.zeros(zone.shape, jnp.float32)

    half = parts // 2
    own_load.wait()
    for part in range(half):
        packed[pl.ds(part * per_source, per_source), :] = jnp.concatenate(
            [own[part], own[part + half]], axis=-1)

    expected = per_group + jnp.where(bottom, 0, 1) + jnp.where(top, 0, 1)
    expected = expected + jnp.where(edge, groups - 1, 0)
    pl.semaphore_wait(barrier, expected)

    def remote(source, target, send, recv, device):
        return pltpu.make_async_remote_copy(
            src_ref=source, dst_ref=target, send_sem=send, recv_sem=recv,
            device_id=device, device_id_type=pl.DeviceIdType.MESH)

    count = HALO - 1

    def stiff_up():
        return remote(stiff.at[:, pl.ds(TILE + rows - count, count)],
                      stiff.at[:, pl.ds(TILE - count, count)],
                      up_send.at[levels], up_recv.at[levels], at(member, tile + 1))

    def stiff_down():
        return remote(stiff.at[:, pl.ds(TILE, HALO)], stiff.at[:, pl.ds(TILE + rows, HALO)],
                      down_send.at[levels], down_recv.at[levels], at(member, tile - 1))

    def up(level):
        return remote(fields.at[:, level, pl.ds(TILE + rows - HALO, HALO)],
                      fields.at[:, level, pl.ds(TILE - HALO, HALO)],
                      up_send.at[level], up_recv.at[level], at(member, tile + 1))

    def down(level):
        return remote(fields.at[:, level, pl.ds(TILE, HALO)],
                      fields.at[:, level, pl.ds(TILE + rows, HALO)],
                      down_send.at[level], down_recv.at[level], at(member, tile - 1))

    def piece(g, source_slot, lane_slot):
        target = jnp.where(tile < sources, tiles - 1, 0)
        return remote(packed, pieces.at[source_slot, lane_slot], piece_send.at[g],
                      piece_recv.at[source_slot, lane_slot], at(group * per_group + g, target))

    def zone_copy(j, level, slot):
        device = at(lax.rem(group + j, groups) * per_group + lane, tile)
        return remote(zone.at[slot, level], zone.at[slot, level], zone_send.at[level, j - 1],
                      zone_recv.at[level, slot], device)

    my_slot = lax.rem(tile, sources)
    for g in range(per_group):
        piece(g, my_slot, lane).start()

    stiff_load.wait()

    @pl.when(tile < tiles - 1)
    def _():
        stiff_up().start()

    @pl.when(tile > 0)
    def _():
        stiff_down().start()

    for level in range(levels):
        loads(level).wait()

        @pl.when(tile < tiles - 1)
        def _():
            up(level).start()

        @pl.when(tile > 0)
        def _():
            down(level).start()

    rows_load.wait()

    def interior(level, carry):
        def load(index):
            at_rows = pl.ds(2 * TILE + TILE * index, TILE)
            return stiff[level, at_rows, :], [fields[f, level, at_rows, :] for f in range(3)]

        def emit(index, values):
            for f in range(3):
                out[0, f, level, pl.ds(TILE + TILE * index, TILE), :] = values[f]

        sweep(load, emit, rows // TILE - 2, None, None)
        return carry

    split = levels // 4
    lax.fori_loop(0, split, interior, 0)

    @pl.when(edge)
    def _():
        first = jnp.where(bottom, ZONE, 0)
        row = lax.broadcasted_iota(jnp.int32, (TILE, LANES), 0)
        wanted = jnp.where(bottom, row, 2 * ZONE - 1 - row)
        for s in range(sources):
            for g in range(per_group):
                piece(0, s, g).wait_recv()
        held = [jnp.zeros((TILE, LANES), jnp.float32) for _ in range(parts)]
        for s in range(sources):
            chosen = [wanted == zone_rows[first + s * per_source + r] for r in range(per_source)]
            for part in range(parts):
                at_rows = pl.ds(part % half * per_source, per_source)
                at_lanes = pl.ds(part // half * width, width)
                block = jnp.concatenate(
                    [pieces[s, g, at_rows, at_lanes] for g in range(per_group)], axis=-1)
                for r in range(per_source):
                    held[part] = jnp.where(chosen[r], block[r:r + 1, :], held[part])
        for part in range(parts):
            zone[group, part % levels, part // levels] = held[part]
        for level in range(levels):
            for j in range(1, groups):
                zone_copy(j, level, group).start()

    lax.fori_loop(split, levels, interior, 0)

    row = lax.broadcasted_iota(jnp.int32, (TILE, columns), 0)
    depth = zone_depth[0].astype(jnp.float32)

    def weights(distance, here):
        distance = distance.astype(jnp.float32)
        ratio = (depth - distance) / depth
        return jnp.where(jnp.logical_and(here, distance < depth), relax_peak * ratio * ratio, 0.0)

    low_weight = weights(row, bottom)
    high_weight = weights(ZONE - 1 - row, top)
    keep = jnp.where(bottom, 0.0, 1.0).astype(jnp.float32)

    @pl.when(tile > 0)
    def _():
        stiff_up().wait_recv()

    @pl.when(tile < tiles - 1)
    def _():
        stiff_down().wait_recv()

    def strips(level, carry):
        @pl.when(tile > 0)
        def _():
            up(level).wait_recv()

        @pl.when(tile < tiles - 1)
        def _():
            down(level).wait_recv()

        @pl.when(edge)
        def _():
            for j in range(1, groups):
                zone_copy(j, level, lax.rem(group + groups - j, groups)).wait_recv()

        def targets():
            return [jnp.concatenate([zone[g, level, f] for g in range(groups)], axis=-1)
                    for f in range(3)]

        def strip(base, weight, keep, emit):
            def load(index):
                at_rows = pl.ds(base + TILE * index, TILE)
                return stiff[level, at_rows, :], [fields[f, level, at_rows, :] for f in range(3)]

            sweep(load, emit, 3, (weight, targets()), keep)

        def emit_low(index, values):
            for f in range(3):
                if index == 1:
                    out[0, f, level, pl.ds(0, TILE), :] = values[f]
                if index == 2:
                    out[0, f, level, pl.ds(TILE, HALO), :] = values[f][:HALO]

        def emit_high(index, values):
            for f in range(3):
                if index == 0:
                    out[0, f, level, pl.ds(rows - TILE - HALO, HALO), :] = values[f][TILE - HALO:]
                if index == 1:
                    out[0, f, level, pl.ds(rows - TILE, TILE), :] = values[f]

        strip(0, low_weight, keep, emit_low)
        strip(rows - TILE, high_weight, None, emit_high)
        return carry

    lax.fori_loop(0, levels, strips, 0)

    @pl.when(tile < tiles - 1)
    def _():
        stiff_up().wait_send()
        for level in range(levels):
            up(level).wait_send()

    @pl.when(tile > 0)
    def _():
        stiff_down().wait_send()
        for level in range(levels):
            down(level).wait_send()

    for g in range(per_group):
        piece(g, my_slot, lane).wait_send()

    @pl.when(edge)
    def _():
        for level in range(levels):
            for j in range(1, groups):
                zone_copy(j, level, group).wait_send()


def body(state, stiffness, driver, zone_rows, zone_depth):
    members = lax.axis_size("member")
    tiles = lax.axis_size("tile")
    levels, rows, columns = stiffness.shape
    driver = jnp.transpose(driver, (1, 0, 2))
    parts, per_source, width = driver.shape
    packed = (parts // 2 * per_source, 2 * width)
    per_group = LANES // width
    groups = members // per_group
    dma = pltpu.SemaphoreType.DMA
    padded = rows + 2 * TILE
    operands = [pltpu.with_memory_space_constraint(operand, pltpu.HBM)
                for operand in (zone_rows, state, stiffness, driver)]
    return pl.pallas_call(
        functools.partial(kernel, members, tiles),
        out_shape=jax.ShapeDtypeStruct(state.shape, jnp.float32),
        in_specs=[pl.BlockSpec(memory_space=pltpu.SMEM)]
        + [pl.BlockSpec(memory_space=pltpu.HBM)] * 4,
        out_specs=pl.BlockSpec(memory_space=pltpu.VMEM),
        scratch_shapes=[
            pltpu.SMEM(zone_rows.shape, jnp.int32),
            dma,
            pltpu.VMEM((3, levels, padded, columns), jnp.float32),
            pltpu.VMEM((levels, padded, columns), jnp.float32),
            pltpu.VMEM(driver.shape, jnp.float32),
            pltpu.VMEM(packed, jnp.float32),
            pltpu.VMEM((tiles // 2, per_group) + packed, jnp.float32),
            pltpu.VMEM((groups, levels, parts // levels, TILE, LANES), jnp.float32),
            dma((levels,)),
            dma,
            dma,
            dma((levels + 1,)),
            dma((levels + 1,)),
            dma((levels + 1,)),
            dma((levels + 1,)),
            dma((per_group,)),
            dma((tiles // 2, per_group)),
            dma((levels, groups)),
            dma((levels, groups)),
        ],
        compiler_params=pltpu.CompilerParams(
            collective_id=0, has_side_effects=True, vmem_limit_bytes=40 * 2**20),
        name="substeps",
    )(zone_depth, *operands)


def solution(mesh):
    in_specs = (
        P("member", None, None, "tile", None),
        P(None, "tile", None),
        P("tile", None, "member"),
        P(),
        P("member"),
    )
    out_specs = P("member", None, None, "tile", None)
    return jax.shard_map(body, mesh=mesh, in_specs=in_specs, out_specs=out_specs, check_vma=False)
```

```python
import functools

import jax
import jax.numpy as jnp
from jax import lax
from jax.experimental import pallas as pl
from jax.experimental.pallas import tpu as pltpu
from jax.sharding import PartitionSpec as P

ZONE = 8
SUBSTEPS = 3
HALO = 3
TILE = 8
LANES = 128

relax_peak = 0.9


def rotated(field, amount, axis):
    return pltpu.roll(field, amount % field.shape[axis], axis)


def sweep(load, emit, tiles, relax, outside):
    columns = None
    pending = [None] * SUBSTEPS

    def finish(stage, above):
        index, stiff, new_pressure, along_x, new_y = pending[stage]
        row = lax.broadcasted_iota(jnp.int32, new_pressure.shape, 0)
        turned = rotated(new_pressure, -1, 0)
        if above is not None:
            turned = jnp.where(row == TILE - 1, rotated(above, -1, 0), turned)
        new_x = along_x - (turned - new_pressure)
        fields = [new_pressure, new_x, new_y]
        if relax is not None and index == 1:
            weight, targets = relax
            fields = [f + weight * (b - f) for f, b in zip(fields, targets)]
        if outside and index == 0:
            fields[1] = jnp.zeros_like(new_x)
        push(stage + 1, index, stiff, fields)

    def push(stage, index, stiff, fields):
        if stage == SUBSTEPS:
            emit(index, fields)
            return
        pressure, along_x, along_y = fields
        row = lax.broadcasted_iota(jnp.int32, pressure.shape, 0)
        turned = rotated(along_x, 1, 0)
        before = pending[stage]
        if before is not None:
            turned = jnp.where(row == 0, rotated(before[3], 1, 0), turned)
        flow = (along_x - turned) + (along_y - rotated(along_y, 1, 1))
        new_pressure = pressure - stiff * flow
        new_y = along_y - (rotated(new_pressure, -1, 1) - new_pressure)
        if before is not None:
            finish(stage, new_pressure)
        pending[stage] = (index, stiff, new_pressure, along_x, new_y)

    for index in range(tiles):
        stiff, fields = load(index)
        push(0, index, stiff, fields)
    for stage in range(SUBSTEPS):
        finish(stage, None)


def kernel(members, tiles, zone_depth, zone_rows_hbm, state, stiffness, driver, out,
           zone_rows, rows_sem, fields, stiff, own, packed, pieces, zone,
           load_sem, stiff_sem, own_sem,
           up_send, up_recv, down_send, down_recv, piece_send, piece_recv, zone_send, zone_recv):
    levels, rows, columns = stiffness.shape
    parts, per_source, width = driver.shape
    per_group = LANES // width
    groups = members // per_group
    sources = tiles // 2
    member = lax.axis_index("member")
    tile = lax.axis_index("tile")
    bottom = tile == 0
    top = tile == tiles - 1
    edge = jnp.logical_or(bottom, top)
    group = member // per_group
    lane = member % per_group

    def at(member_to, tile_to):
        return {"member": member_to, "tile": tile_to}

    def loads(level):
        return pltpu.make_async_copy(
            state.at[0, :, level], fields.at[:, level, pl.ds(TILE, rows)], load_sem.at[level])

    stiff_load = pltpu.make_async_copy(stiffness, stiff.at[:, pl.ds(TILE, rows)], stiff_sem)

    barrier = pltpu.get_barrier_semaphore()

    def greet(device):
        pl.semaphore_signal(barrier, inc=1, device_id=device, device_id_type=pl.DeviceIdType.MESH)

    @pl.when(tile > 0)
    def _():
        greet(at(member, tile - 1))

    @pl.when(tile < tiles - 1)
    def _():
        greet(at(member, tile + 1))

    @pl.when(edge)
    def _():
        first = jnp.where(bottom, sources, 0)
        for s in range(sources):
            for g in range(per_group):
                greet(at(group * per_group + g, first + s))
        for j in range(1, groups):
            greet(at(lax.rem(group + j, groups) * per_group + lane, tile))

    own_load = pltpu.make_async_copy(driver, own, own_sem)
    rows_load = pltpu.make_async_copy(zone_rows_hbm, zone_rows, rows_sem)
    own_load.start()
    stiff_load.start()
    for level in range(levels):
        loads(level).start()
    rows_load.start()

    @pl.when(bottom)
    def _():
        fields[:, :, :TILE, :] = jnp.zeros((3, levels, TILE, columns), jnp.float32)
        stiff[:, :TILE, :] = jnp.zeros((levels, TILE, columns), jnp.float32)

    @pl.when(top)
    def _():
        fields[:, :, TILE + rows:, :] = jnp.zeros((3, levels, TILE, columns), jnp.float32)
        stiff[:, TILE + rows:, :] = jnp.zeros((levels, TILE, columns), jnp.float32)

    half = parts // 2
    own_load.wait()
    for part in range(half):
        packed[pl.ds(part * per_source, per_source), :] = jnp.concatenate(
            [own[part], own[part + half]], axis=-1)

    expected = per_group + jnp.where(bottom, 0, 1) + jnp.where(top, 0, 1)
    expected = expected + jnp.where(edge, groups - 1, 0)
    pl.semaphore_wait(barrier, expected)

    def remote(source, target, send, recv, device):
        return pltpu.make_async_remote_copy(
            src_ref=source, dst_ref=target, send_sem=send, recv_sem=recv,
            device_id=device, device_id_type=pl.DeviceIdType.MESH)

    count = HALO - 1

    def stiff_up():
        return remote(stiff.at[:, pl.ds(TILE + rows - count, count)],
                      stiff.at[:, pl.ds(TILE - count, count)],
                      up_send.at[levels], up_recv.at[levels], at(member, tile + 1))

    def stiff_down():
        return remote(stiff.at[:, pl.ds(TILE, HALO)], stiff.at[:, pl.ds(TILE + rows, HALO)],
                      down_send.at[levels], down_recv.at[levels], at(member, tile - 1))

    def up(level):
        return remote(fields.at[:, level, pl.ds(TILE + rows - HALO, HALO)],
                      fields.at[:, level, pl.ds(TILE - HALO, HALO)],
                      up_send.at[level], up_recv.at[level], at(member, tile + 1))

    def down(level):
        return remote(fields.at[:, level, pl.ds(TILE, HALO)],
                      fields.at[:, level, pl.ds(TILE + rows, HALO)],
                      down_send.at[level], down_recv.at[level], at(member, tile - 1))

    def piece(g, source_slot, lane_slot):
        target = jnp.where(tile < sources, tiles - 1, 0)
        return remote(packed, pieces.at[source_slot, lane_slot], piece_send.at[g],
                      piece_recv.at[source_slot, lane_slot], at(group * per_group + g, target))

    def zone_copy(j, slot):
        device = at(lax.rem(group + j, groups) * per_group + lane, tile)
        return remote(zone.at[slot], zone.at[slot], zone_send.at[j - 1], zone_recv.at[slot], device)

    my_slot = lax.rem(tile, sources)
    for g in range(per_group):
        piece(g, my_slot, lane).start()

    stiff_load.wait()

    @pl.when(tile < tiles - 1)
    def _():
        stiff_up().start()

    @pl.when(tile > 0)
    def _():
        stiff_down().start()

    for level in range(levels):
        loads(level).wait()

        @pl.when(tile < tiles - 1)
        def _():
            up(level).start()

        @pl.when(tile > 0)
        def _():
            down(level).start()

    rows_load.wait()

    def interior(level, carry):
        def load(index):
            at_rows = pl.ds(2 * TILE + TILE * index, TILE)
            return stiff[level, at_rows, :], [fields[f, level, at_rows, :] for f in range(3)]

        def emit(index, values):
            for f in range(3):
                out[0, f, level, pl.ds(TILE + TILE * index, TILE), :] = values[f]

        sweep(load, emit, rows // TILE - 2, None, False)
        return carry

    split = levels // 4
    lax.fori_loop(0, split, interior, 0)

    @pl.when(edge)
    def _():
        first = jnp.where(bottom, ZONE, 0)
        row = lax.broadcasted_iota(jnp.int32, (TILE, LANES), 0)
        wanted = jnp.where(bottom, row, 2 * ZONE - 1 - row)
        for s in range(sources):
            for g in range(per_group):
                piece(0, s, g).wait_recv()
        held = [jnp.zeros((TILE, LANES), jnp.float32) for _ in range(parts)]
        for s in range(sources):
            chosen = [wanted == zone_rows[first + s * per_source + r] for r in range(per_source)]
            for part in range(parts):
                at_rows = pl.ds(part % half * per_source, per_source)
                at_lanes = pl.ds(part // half * width, width)
                block = jnp.concatenate(
                    [pieces[s, g, at_rows, at_lanes] for g in range(per_group)], axis=-1)
                for r in range(per_source):
                    held[part] = jnp.where(chosen[r], block[r:r + 1, :], held[part])
        for part in range(parts):
            zone[group, part % levels, part // levels] = held[part]
        for j in range(1, groups):
            zone_copy(j, group).start()

    lax.fori_loop(split, levels, interior, 0)

    row = lax.broadcasted_iota(jnp.int32, (TILE, columns), 0)
    depth = zone_depth[0].astype(jnp.float32)

    def weights(distance, here):
        distance = distance.astype(jnp.float32)
        ratio = (depth - distance) / depth
        return jnp.where(jnp.logical_and(here, distance < depth), relax_peak * ratio * ratio, 0.0)

    low_weight = weights(row, bottom)
    high_weight = weights(ZONE - 1 - row, top)
    def strip(level, base, weight, outside, emit):
        def load(index):
            at_rows = pl.ds(base + TILE * index, TILE)
            return stiff[level, at_rows, :], [fields[f, level, at_rows, :] for f in range(3)]

        relax = None
        if weight is not None:
            relax = (weight, [jnp.concatenate([zone[g, level, f] for g in range(groups)], axis=-1)
                              for f in range(3)])
        sweep(load, emit, 3, relax, outside)

    def low_strip(level, weight):
        def emit(index, values):
            for f in range(3):
                if index == 1:
                    out[0, f, level, pl.ds(0, TILE), :] = values[f]
                if index == 2:
                    out[0, f, level, pl.ds(TILE, HALO), :] = values[f][:HALO]

        strip(level, 0, weight, weight is not None, emit)

    def high_strip(level, weight):
        def emit(index, values):
            for f in range(3):
                if index == 0:
                    out[0, f, level, pl.ds(rows - TILE - HALO, HALO), :] = values[f][TILE - HALO:]
                if index == 1:
                    out[0, f, level, pl.ds(rows - TILE, TILE), :] = values[f]

        strip(level, rows - TILE, weight, False, emit)

    def zone_arrival():
        for j in range(1, groups):
            zone_copy(j, lax.rem(group + groups - j, groups)).wait_recv()

    def low_arrival(level):
        up(level).wait_recv()

    def high_arrival(level):
        down(level).wait_recv()

    def strips(together, arrivals, one):
        def several(index, carry):
            chosen = [index * together + k for k in range(together)]
            for level in chosen:
                for arrival in arrivals:
                    arrival(level)
            for level in chosen:
                one(level)
            return carry

        lax.fori_loop(0, levels // together, several, 0)

    pair = 2 if levels % 2 == 0 else 1

    @pl.when(bottom)
    def _():
        stiff_down().wait_recv()
        strips(pair, [high_arrival], lambda level: high_strip(level, None))
        zone_arrival()
        strips(levels, [], lambda level: low_strip(level, low_weight))

    @pl.when(top)
    def _():
        stiff_up().wait_recv()
        strips(pair, [low_arrival], lambda level: low_strip(level, None))
        zone_arrival()
        strips(levels, [], lambda level: high_strip(level, high_weight))

    @pl.when(jnp.logical_not(edge))
    def _():
        def both(level):
            low_strip(level, None)
            high_strip(level, None)

        stiff_up().wait_recv()
        stiff_down().wait_recv()
        strips(1, [low_arrival, high_arrival], both)

    @pl.when(tile < tiles - 1)
    def _():
        stiff_up().wait_send()
        for level in range(levels):
            up(level).wait_send()

    @pl.when(tile > 0)
    def _():
        stiff_down().wait_send()
        for level in range(levels):
            down(level).wait_send()

    for g in range(per_group):
        piece(g, my_slot, lane).wait_send()

    @pl.when(edge)
    def _():
        for j in range(1, groups):
            zone_copy(j, group).wait_send()


def body(state, stiffness, driver, zone_rows, zone_depth):
    members = lax.axis_size("member")
    tiles = lax.axis_size("tile")
    levels, rows, columns = stiffness.shape
    driver = jnp.transpose(driver, (1, 0, 2))
    parts, per_source, width = driver.shape
    packed = (parts // 2 * per_source, 2 * width)
    per_group = LANES // width
    groups = members // per_group
    dma = pltpu.SemaphoreType.DMA
    padded = rows + 2 * TILE
    operands = [pltpu.with_memory_space_constraint(operand, pltpu.HBM)
                for operand in (zone_rows, state, stiffness, driver)]
    return pl.pallas_call(
        functools.partial(kernel, members, tiles),
        out_shape=jax.ShapeDtypeStruct(state.shape, jnp.float32),
        in_specs=[pl.BlockSpec(memory_space=pltpu.SMEM)]
        + [pl.BlockSpec(memory_space=pltpu.HBM)] * 4,
        out_specs=pl.BlockSpec(memory_space=pltpu.VMEM),
        scratch_shapes=[
            pltpu.SMEM(zone_rows.shape, jnp.int32),
            dma,
            pltpu.VMEM((3, levels, padded, columns), jnp.float32),
            pltpu.VMEM((levels, padded, columns), jnp.float32),
            pltpu.VMEM(driver.shape, jnp.float32),
            pltpu.VMEM(packed, jnp.float32),
            pltpu.VMEM((tiles // 2, per_group) + packed, jnp.float32),
            pltpu.VMEM((groups, levels, parts // levels, TILE, LANES), jnp.float32),
            dma((levels,)),
            dma,
            dma,
            dma((levels + 1,)),
            dma((levels + 1,)),
            dma((levels + 1,)),
            dma((levels + 1,)),
            dma((per_group,)),
            dma((tiles // 2, per_group)),
            dma((groups,)),
            dma((groups,)),
        ],
        compiler_params=pltpu.CompilerParams(
            collective_id=0, has_side_effects=True, vmem_limit_bytes=40 * 2**20),
        name="substeps",
    )(zone_depth, *operands)


def solution(mesh):
    in_specs = (
        P("member", None, None, "tile", None),
        P(None, "tile", None),
        P("tile", None, "member"),
        P(),
        P("member"),
    )
    out_specs = P("member", None, None, "tile", None)
    return jax.shard_map(body, mesh=mesh, in_specs=in_specs, out_specs=out_specs, check_vma=False)
```

```python
import functools

import jax
import jax.numpy as jnp
from jax import lax
from jax.experimental import pallas as pl
from jax.experimental.pallas import tpu as pltpu
from jax.sharding import PartitionSpec as P

ZONE = 8
SUBSTEPS = 3
HALO = 3
TILE = 8
LANES = 128

relax_peak = 0.9


def rotated(field, amount, axis):
    return pltpu.roll(field, amount % field.shape[axis], axis)


def sweep(load, emit, tiles, relax, zone_index):
    columns = None
    pending = [None] * SUBSTEPS

    def finish(stage, above):
        index, stiff, new_pressure, along_x, new_y = pending[stage]
        row = lax.broadcasted_iota(jnp.int32, new_pressure.shape, 0)
        turned = rotated(new_pressure, -1, 0)
        if above is not None:
            turned = jnp.where(row == TILE - 1, rotated(above, -1, 0), turned)
        elif zone_index == tiles - 1:
            turned = jnp.where(row == TILE - 1, 0.0, turned)
        new_x = along_x - (turned - new_pressure)
        fields = [new_pressure, new_x, new_y]
        if index == zone_index:
            weight, targets = relax
            fields = [f + weight * (b - f) for f, b in zip(fields, targets)]
        push(stage + 1, index, stiff, fields)

    def push(stage, index, stiff, fields):
        if stage == SUBSTEPS:
            emit(index, fields)
            return
        pressure, along_x, along_y = fields
        row = lax.broadcasted_iota(jnp.int32, pressure.shape, 0)
        turned = rotated(along_x, 1, 0)
        before = pending[stage]
        if before is not None:
            turned = jnp.where(row == 0, rotated(before[3], 1, 0), turned)
        elif zone_index == 0:
            turned = jnp.where(row == 0, 0.0, turned)
        flow = (along_x - turned) + (along_y - rotated(along_y, 1, 1))
        new_pressure = pressure - stiff * flow
        new_y = along_y - (rotated(new_pressure, -1, 1) - new_pressure)
        if before is not None:
            finish(stage, new_pressure)
        pending[stage] = (index, stiff, new_pressure, along_x, new_y)

    for index in range(tiles):
        stiff, fields = load(index)
        push(0, index, stiff, fields)
    for stage in range(SUBSTEPS):
        finish(stage, None)


def kernel(members, tiles, zone_depth, zone_rows_hbm, state, stiffness, driver, out,
           zone_rows, rows_sem, fields, stiff, own, packed, pieces, zone,
           load_sem, stiff_sem, own_sem,
           up_send, up_recv, down_send, down_recv, piece_send, piece_recv, zone_send, zone_recv):
    levels, rows, columns = stiffness.shape
    parts, per_source, width = driver.shape
    per_group = LANES // width
    groups = members // per_group
    sources = tiles // 2
    member = lax.axis_index("member")
    tile = lax.axis_index("tile")
    bottom = tile == 0
    top = tile == tiles - 1
    edge = jnp.logical_or(bottom, top)
    group = member // per_group
    lane = member % per_group

    def at(member_to, tile_to):
        return {"member": member_to, "tile": tile_to}

    def loads(level):
        return pltpu.make_async_copy(
            state.at[0, :, level], fields.at[:, level, pl.ds(TILE, rows)], load_sem.at[level])

    stiff_load = pltpu.make_async_copy(stiffness, stiff.at[:, pl.ds(TILE, rows)], stiff_sem)

    barrier = pltpu.get_barrier_semaphore()

    def greet(device):
        pl.semaphore_signal(barrier, inc=1, device_id=device, device_id_type=pl.DeviceIdType.MESH)

    @pl.when(tile > 0)
    def _():
        greet(at(member, tile - 1))

    @pl.when(tile < tiles - 1)
    def _():
        greet(at(member, tile + 1))

    @pl.when(edge)
    def _():
        first = jnp.where(bottom, sources, 0)
        for s in range(sources):
            for g in range(per_group):
                greet(at(group * per_group + g, first + s))
        for j in range(1, groups):
            greet(at(lax.rem(group + j, groups) * per_group + lane, tile))

    own_load = pltpu.make_async_copy(driver, own, own_sem)
    rows_load = pltpu.make_async_copy(zone_rows_hbm, zone_rows, rows_sem)
    own_load.start()
    stiff_load.start()
    for level in range(levels):
        loads(level).start()
    rows_load.start()

    half = parts // 2
    own_load.wait()
    for part in range(half):
        packed[pl.ds(part * per_source, per_source), :] = jnp.concatenate(
            [own[part], own[part + half]], axis=-1)

    expected = per_group + jnp.where(bottom, 0, 1) + jnp.where(top, 0, 1)
    expected = expected + jnp.where(edge, groups - 1, 0)
    pl.semaphore_wait(barrier, expected)

    def remote(source, target, send, recv, device):
        return pltpu.make_async_remote_copy(
            src_ref=source, dst_ref=target, send_sem=send, recv_sem=recv,
            device_id=device, device_id_type=pl.DeviceIdType.MESH)

    count = HALO - 1

    def stiff_up():
        return remote(stiff.at[:, pl.ds(TILE + rows - count, count)],
                      stiff.at[:, pl.ds(TILE - count, count)],
                      up_send.at[levels], up_recv.at[levels], at(member, tile + 1))

    def stiff_down():
        return remote(stiff.at[:, pl.ds(TILE, HALO)], stiff.at[:, pl.ds(TILE + rows, HALO)],
                      down_send.at[levels], down_recv.at[levels], at(member, tile - 1))

    def up(level):
        return remote(fields.at[:, level, pl.ds(TILE + rows - HALO, HALO)],
                      fields.at[:, level, pl.ds(TILE - HALO, HALO)],
                      up_send.at[level], up_recv.at[level], at(member, tile + 1))

    def down(level):
        return remote(fields.at[:, level, pl.ds(TILE, HALO)],
                      fields.at[:, level, pl.ds(TILE + rows, HALO)],
                      down_send.at[level], down_recv.at[level], at(member, tile - 1))

    def piece(g, source_slot, lane_slot):
        target = jnp.where(tile < sources, tiles - 1, 0)
        return remote(packed, pieces.at[source_slot, lane_slot], piece_send.at[g],
                      piece_recv.at[source_slot, lane_slot], at(group * per_group + g, target))

    def zone_copy(j, slot):
        device = at(lax.rem(group + j, groups) * per_group + lane, tile)
        return remote(zone.at[slot], zone.at[slot], zone_send.at[j - 1], zone_recv.at[slot], device)

    my_slot = lax.rem(tile, sources)
    for g in range(per_group):
        piece(g, my_slot, lane).start()

    stiff_load.wait()

    @pl.when(tile < tiles - 1)
    def _():
        stiff_up().start()

    @pl.when(tile > 0)
    def _():
        stiff_down().start()

    for level in range(levels):
        loads(level).wait()

        @pl.when(tile < tiles - 1)
        def _():
            up(level).start()

        @pl.when(tile > 0)
        def _():
            down(level).start()

    rows_load.wait()

    def interior(level, carry):
        def load(index):
            at_rows = pl.ds(2 * TILE + TILE * index, TILE)
            return stiff[level, at_rows, :], [fields[f, level, at_rows, :] for f in range(3)]

        def emit(index, values):
            for f in range(3):
                out[0, f, level, pl.ds(TILE + TILE * index, TILE), :] = values[f]

        sweep(load, emit, rows // TILE - 2, None, None)
        return carry

    split = levels // 4
    lax.fori_loop(0, split, interior, 0)

    @pl.when(edge)
    def _():
        first = jnp.where(bottom, ZONE, 0)
        row = lax.broadcasted_iota(jnp.int32, (TILE, LANES), 0)
        wanted = jnp.where(bottom, row, 2 * ZONE - 1 - row)
        for s in range(sources):
            for g in range(per_group):
                piece(0, s, g).wait_recv()
        held = [jnp.zeros((TILE, LANES), jnp.float32) for _ in range(parts)]
        for s in range(sources):
            chosen = [wanted == zone_rows[first + s * per_source + r] for r in range(per_source)]
            for part in range(parts):
                at_rows = pl.ds(part % half * per_source, per_source)
                at_lanes = pl.ds(part // half * width, width)
                block = jnp.concatenate(
                    [pieces[s, g, at_rows, at_lanes] for g in range(per_group)], axis=-1)
                for r in range(per_source):
                    held[part] = jnp.where(chosen[r], block[r:r + 1, :], held[part])
        for part in range(parts):
            zone[group, part % levels, part // levels] = held[part]
        for j in range(1, groups):
            zone_copy(j, group).start()

    lax.fori_loop(split, levels, interior, 0)

    row = lax.broadcasted_iota(jnp.int32, (TILE, columns), 0)
    depth = zone_depth[0].astype(jnp.float32)

    def weights(distance, here):
        distance = distance.astype(jnp.float32)
        ratio = (depth - distance) / depth
        return jnp.where(jnp.logical_and(here, distance < depth), relax_peak * ratio * ratio, 0.0)

    low_weight = weights(row, bottom)
    high_weight = weights(ZONE - 1 - row, top)
    def strip(level, base, weight, zone_index, emit):
        def load(index):
            at_rows = pl.ds(base + TILE * index, TILE)
            return stiff[level, at_rows, :], [fields[f, level, at_rows, :] for f in range(3)]

        relax = None
        if weight is not None:
            relax = (weight, [jnp.concatenate([zone[g, level, f] for g in range(groups)], axis=-1)
                              for f in range(3)])
        sweep(load, emit, 3 if weight is None else 2, relax, zone_index)

    def low_strip(level, weight):
        skip = 0 if weight is None else 1

        def emit(index, values):
            index = index + skip
            for f in range(3):
                if index == 1:
                    out[0, f, level, pl.ds(0, TILE), :] = values[f]
                if index == 2:
                    out[0, f, level, pl.ds(TILE, HALO), :] = values[f][:HALO]

        strip(level, TILE * skip, weight, None if weight is None else 0, emit)

    def high_strip(level, weight):
        def emit(index, values):
            for f in range(3):
                if index == 0:
                    out[0, f, level, pl.ds(rows - TILE - HALO, HALO), :] = values[f][TILE - HALO:]
                if index == 1:
                    out[0, f, level, pl.ds(rows - TILE, TILE), :] = values[f]

        strip(level, rows - TILE, weight, None if weight is None else 1, emit)

    def zone_arrival():
        for j in range(1, groups):
            zone_copy(j, lax.rem(group + groups - j, groups)).wait_recv()

    def low_arrival(level):
        up(level).wait_recv()

    def high_arrival(level):
        down(level).wait_recv()

    def strips(together, arrivals, one):
        def several(index, carry):
            chosen = [index * together + k for k in range(together)]
            for level in chosen:
                for arrival in arrivals:
                    arrival(level)
            for level in chosen:
                one(level)
            return carry

        lax.fori_loop(0, levels // together, several, 0)

    pair = 2 if levels % 2 == 0 else 1

    @pl.when(bottom)
    def _():
        stiff_down().wait_recv()
        strips(pair, [high_arrival], lambda level: high_strip(level, None))
        zone_arrival()
        strips(levels, [], lambda level: low_strip(level, low_weight))

    @pl.when(top)
    def _():
        stiff_up().wait_recv()
        strips(pair, [low_arrival], lambda level: low_strip(level, None))
        zone_arrival()
        strips(levels, [], lambda level: high_strip(level, high_weight))

    @pl.when(jnp.logical_not(edge))
    def _():
        def both(level):
            low_strip(level, None)
            high_strip(level, None)

        stiff_up().wait_recv()
        stiff_down().wait_recv()
        strips(1, [low_arrival, high_arrival], both)

    @pl.when(tile < tiles - 1)
    def _():
        stiff_up().wait_send()
        for level in range(levels):
            up(level).wait_send()

    @pl.when(tile > 0)
    def _():
        stiff_down().wait_send()
        for level in range(levels):
            down(level).wait_send()

    for g in range(per_group):
        piece(g, my_slot, lane).wait_send()

    @pl.when(edge)
    def _():
        for j in range(1, groups):
            zone_copy(j, group).wait_send()


def body(state, stiffness, driver, zone_rows, zone_depth):
    members = lax.axis_size("member")
    tiles = lax.axis_size("tile")
    levels, rows, columns = stiffness.shape
    driver = jnp.transpose(driver, (1, 0, 2))
    parts, per_source, width = driver.shape
    packed = (parts // 2 * per_source, 2 * width)
    per_group = LANES // width
    groups = members // per_group
    dma = pltpu.SemaphoreType.DMA
    padded = rows + 2 * TILE
    operands = [pltpu.with_memory_space_constraint(operand, pltpu.HBM)
                for operand in (zone_rows, state, stiffness, driver)]
    return pl.pallas_call(
        functools.partial(kernel, members, tiles),
        out_shape=jax.ShapeDtypeStruct(state.shape, jnp.float32),
        in_specs=[pl.BlockSpec(memory_space=pltpu.SMEM)]
        + [pl.BlockSpec(memory_space=pltpu.HBM)] * 4,
        out_specs=pl.BlockSpec(memory_space=pltpu.VMEM),
        scratch_shapes=[
            pltpu.SMEM(zone_rows.shape, jnp.int32),
            dma,
            pltpu.VMEM((3, levels, padded, columns), jnp.float32),
            pltpu.VMEM((levels, padded, columns), jnp.float32),
            pltpu.VMEM(driver.shape, jnp.float32),
            pltpu.VMEM(packed, jnp.float32),
            pltpu.VMEM((tiles // 2, per_group) + packed, jnp.float32),
            pltpu.VMEM((groups, levels, parts // levels, TILE, LANES), jnp.float32),
            dma((levels,)),
            dma,
            dma,
            dma((levels + 1,)),
            dma((levels + 1,)),
            dma((levels + 1,)),
            dma((levels + 1,)),
            dma((per_group,)),
            dma((tiles // 2, per_group)),
            dma((groups,)),
            dma((groups,)),
        ],
        compiler_params=pltpu.CompilerParams(
            collective_id=0, has_side_effects=True, vmem_limit_bytes=40 * 2**20),
        name="substeps",
    )(zone_depth, *operands)


def solution(mesh):
    in_specs = (
        P("member", None, None, "tile", None),
        P(None, "tile", None),
        P("tile", None, "member"),
        P(),
        P("member"),
    )
    out_specs = P("member", None, None, "tile", None)
    return jax.shard_map(body, mesh=mesh, in_specs=in_specs, out_specs=out_specs, check_vma=False)
```
